32 devices in a mesh: grid: 2 (over y), member: 8 (over z, x), sample: 2 (over core).
Axes of the slice: x: 2, y: 2, z: 4, core: 2. Of those that a mesh axis runs over, the one named last changes fastest.
Arguments:
- hidden_states: bfloat16 [2, 8, 2048, 1024], P('sample', 'member', 'grid'), may hold values from -6 to 6
- targets: float32 [2, 100, 2048], P('sample', None, 'grid'), may hold values from -6 to 6
- area_weight: float32 [2048], P('grid'), may hold values from 0.2 to 2
- var_weight: float32 [100], replicated, may hold values from 0.25 to 4
- weight_in: bfloat16 [1024, 1024], replicated, may hold values from -0.1875 to 0.1875
- bias_in: float32 [1024], replicated, may hold values from -3 to 3
- output_weight: bfloat16 [1024, 100], replicated, may hold values from -0.1875 to 0.1875
- output_bias: float32 [100], replicated, may hold values from -3 to 3
Outputs:
- grad_weight_in: float32 [1024, 1024], P(('grid', 'member'))
- grad_bias_in: float32 [1024], P(('grid', 'member'))
- grad_weight_out: float32 [1024, 100], P(('grid', 'member'))
The draws below stay inside these ranges and needn't reach their ends.
All inputs are finite; a program needn't handle non-finite values.
Results may differ from the reference program's by a relative error of at most 0.0058.
Values may be sent and summed in bfloat16 or wider, within the bound.
A program may use at most 64 MiB of HBM per device.

```python
import math
import jax
import jax.numpy as jnp
from jax import lax

D = 1024
FF = 1024
OUTPUT_FIELDS = 100
GRID_COUNT = 2048
ENSEMBLE_SIZE = 8
SAMPLE_COUNT = 2


def strengthened(values, key, source, target, blocks, factor):
    def block_of(dim):
        return (jnp.arange(values.shape[dim]) // (values.shape[dim] // blocks)).reshape((-1,) + (1,) * (values.ndim - 1 - dim))

    first = jax.random.permutation(key, blocks)[block_of(target)]
    second = (block_of(target) + blocks // 2) % blocks
    return jnp.where((block_of(source) == first) | (block_of(source) == second), factor * values, values)


def block_levels(stream_key, extent, cuts, smallest, high):
    level = 1.0
    for dim, parts in cuts:
        steps = jax.random.uniform(jax.random.fold_in(jax.random.fold_in(stream_key, 6), dim), (parts,), jnp.float32, smallest / len(cuts), high / len(cuts))
        level = level * jnp.repeat(jnp.exp(steps), extent[dim] // parts).reshape((-1,) + (1,) * (len(extent) - 1 - dim))
    return level


def normal_values(rng, shape, deviation, bound, cuts=(), held_as=jnp.bfloat16):
    drawn = deviation * jax.random.normal(rng, shape, jnp.float32)
    if cuts:
        drawn = drawn * block_levels(rng, shape, cuts, -0.22, 0.18)
    return jnp.clip(drawn, -bound, bound).astype(held_as)


def gaussian_with(key, dims, width, bound, pieces, heavy, dtype=jnp.bfloat16):
    result = width * jax.random.normal(key, dims, jnp.float32)
    if pieces:
        result = result * block_levels(key, dims, pieces, -0.22, 0.18)
    return jnp.clip(strengthened(result, jax.random.fold_in(key, 3), *heavy), -bound, bound).astype(dtype)


def setup_inputs(seed: int = 0) -> dict:
    splits = jax.random.split(jax.random.key(seed), 9)
    return {
        "hidden_states": gaussian_with(splits[0], (SAMPLE_COUNT, ENSEMBLE_SIZE, GRID_COUNT, D), 1.0, 6.0, ((0, 2), (1, 8), (2, 2)), (2, 3, 2, 2.0)),
        "targets": normal_values(splits[1], (SAMPLE_COUNT, OUTPUT_FIELDS, GRID_COUNT), 1.0, 6.0, ((0, 2), (2, 2)), jnp.float32),
        "area_weight": jnp.clip(jnp.exp(math.log(2.0) - 2.3025851 * jax.random.uniform(splits[2], (GRID_COUNT,), jnp.float32) ** block_levels(splits[2], (GRID_COUNT,), ((0, 2),), -0.2, 0.2)), 0.2, 2.0),
        "var_weight": jnp.clip(jnp.exp(jax.random.uniform(splits[3], (OUTPUT_FIELDS,), jnp.float32, math.log(0.25), math.log(4.0))), 0.25, 4.0),
        "weight_in": normal_values(splits[4], (D, FF), D ** -0.5, 0.1875),
        "bias_in": normal_values(splits[5], (FF,), 0.5, 3.0, (), jnp.float32),
        "output_weight": normal_values(splits[6], (FF, OUTPUT_FIELDS), FF ** -0.5, 0.1875),
        "output_bias": normal_values(splits[7], (OUTPUT_FIELDS,), 0.5, 3.0, (), jnp.float32),
    }


smoothing = 0.01
alpha_fair = 0.95

def softened_slope(value):
    return value * lax.rsqrt(value * value + smoothing)

def forward(inputs, weight_in, bias_in, output_weight, output_bias):
    pre_activation = jnp.dot(inputs, weight_in, preferred_element_type=jnp.float32) + bias_in
    hidden_activation = jax.nn.gelu(pre_activation).astype(jnp.bfloat16)
    member_prediction = lax.dot_general(output_weight, hidden_activation, (((0,), (1,)), ((), ())), preferred_element_type=jnp.float32) + output_bias[:, None]
    return (pre_activation, hidden_activation, member_prediction)

def reference(hidden_states, targets, area_weight, var_weight, weight_in, bias_in, output_weight, output_bias):
    flattened_input = hidden_states.reshape(SAMPLE_COUNT * ENSEMBLE_SIZE, GRID_COUNT, D)

    def forward_pass_step(carry, inputs):
        return (carry, forward(inputs, weight_in, bias_in, output_weight, output_bias)[2])
    unused_value, ensemble_predictions = lax.scan(forward_pass_step, jnp.zeros((), jnp.float32), flattened_input)
    ensemble_predictions = ensemble_predictions.reshape(SAMPLE_COUNT, ENSEMBLE_SIZE, OUTPUT_FIELDS, GRID_COUNT)

    def pairwise_step(member_index, running_total):
        partner_member = lax.dynamic_slice_in_dim(ensemble_predictions, member_index, 1, 1)
        return running_total + softened_slope(ensemble_predictions - partner_member)
    pairwise_total = lax.fori_loop(0, ENSEMBLE_SIZE, pairwise_step, jnp.zeros(ensemble_predictions.shape, jnp.float32))
    eps_fair = (1.0 - alpha_fair) / ENSEMBLE_SIZE
    pairwise_coefficient = (1.0 - eps_fair) / (ENSEMBLE_SIZE * (ENSEMBLE_SIZE - 1))
    loss_scale = ENSEMBLE_SIZE / jnp.sqrt(jnp.float32(SAMPLE_COUNT * GRID_COUNT))
    latitude_weighting = loss_scale * area_weight[None, :] * var_weight[:, None]
    prediction_gradient = latitude_weighting[None, None] * (softened_slope(ensemble_predictions - targets[:, None]) / ENSEMBLE_SIZE - pairwise_coefficient * pairwise_total)
    prediction_gradient = prediction_gradient.astype(jnp.bfloat16).reshape(SAMPLE_COUNT * ENSEMBLE_SIZE, OUTPUT_FIELDS, GRID_COUNT)

    def backward_step(carry, items):
        inputs, gradient_rows = items
        pre_activation, hidden_activation, unused_value = forward(inputs, weight_in, bias_in, output_weight, output_bias)
        act_grad = lax.dot_general(gradient_rows, output_weight, (((0,), (1,)), ((), ())), preferred_element_type=jnp.float32)
        unused_value, gelu_back = jax.vjp(jax.nn.gelu, pre_activation)
        preact_grad_f = gelu_back(act_grad)[0]
        preact_grad = preact_grad_f.astype(jnp.bfloat16)
        grad_in = lax.dot_general(inputs, preact_grad, (((0,), (0,)), ((), ())), preferred_element_type=jnp.float32)
        grad_out = lax.dot_general(hidden_activation, gradient_rows, (((0,), (1,)), ((), ())), preferred_element_type=jnp.float32)
        return ((carry[0] + grad_in, carry[1] + lax.optimization_barrier(jnp.sum(preact_grad_f, axis=0)), carry[2] + grad_out), None)
    start_offset = (jnp.zeros((D, FF), jnp.float32), jnp.zeros((FF,), jnp.float32), jnp.zeros((FF, OUTPUT_FIELDS), jnp.float32))
    parameter_gradients, unused_value = lax.scan(backward_step, start_offset, (flattened_input, prediction_gradient))
    return (parameter_gradients[0], parameter_gradients[1], parameter_gradients[2])
```

```python
import functools
import math

import jax
import jax.numpy as jnp
from jax import lax
from jax.experimental import pallas as pl
from jax.experimental.pallas import tpu as pltpu
from jax.sharding import PartitionSpec as P

smoothing = 0.01
alpha_fair = 0.95
LANES = 128
MEMBER_ROWS = 4
GELU_C = math.sqrt(2.0 / math.pi)
GELU_A = 0.044715
MESH = pl.DeviceIdType.MESH
F32 = jnp.float32
BF16 = jnp.bfloat16
ORDERS = ("xyz", "yxz", "xyz", "yxz", "yxz")


def softened_slope(value):
    return value * lax.rsqrt(value * value + smoothing)


def kernel(
    sizes, chunk_axes,
    x_hbm, t_hbm, area_ref, var_ref, win_hbm, bin_ref, wout_hbm, bout_ref,
    gin_ref, gbias_ref, gout_ref,
    x_v, xt_v, win_v, wout_v, w128, w128t, tv, t128, tt,
    pre, act, pg, bias_acc, fsend, frecv, gsend, grecv, goutt,
    csend, crecv, own, s1, r1, s2, r2, s3, r3, acc, fin_s, fin_r,
    in_sem, f_ss, f_rs, g_ss, g_rs, c_ss, c_rs, r_ss, r_rs, e_ss, e_rs,
):
    G, MZ, MX, S, R = sizes
    M = MZ * MX
    points, depth = x_v.shape
    width = win_v.shape[1]
    fields = wout_v.shape[1]
    per = points // M
    step = points // MZ
    half = width // S
    grid = lax.axis_index("grid")
    me = lax.axis_index("member")
    core = lax.axis_index("sample")
    mz, mx = me // MX, me % MX
    other = 1 - core

    pending = []

    def fetch(src, dst, n):
        copy = pltpu.make_async_copy(src, dst, in_sem.at[n])
        copy.start()
        return copy

    def rows_of(i):
        return pl.multiple_of(lax.rem(mz + 1 + i, MZ) * step, step)

    get_win = fetch(win_hbm, win_v, 0)
    get_x = [
        fetch(x_hbm.at[0, 0, pl.ds(rows_of(i), step)], x_v.at[pl.ds(rows_of(i), step)], 1 + i)
        for i in range(MZ)
    ]
    get_wout = fetch(wout_hbm, wout_v, 1 + MZ)
    get_t = fetch(t_hbm.at[0], tv, 2 + MZ)

    barrier = pltpu.get_barrier_semaphore()
    for s in range(1, M):
        pl.semaphore_signal(barrier, inc=1, device_id={"member": lax.rem(me + s, M)}, device_id_type=MESH)
    for s in range(1, G):
        pl.semaphore_signal(barrier, inc=1, device_id={"grid": lax.rem(grid + s, G)}, device_id_type=MESH)
    pl.semaphore_signal(barrier, inc=1, device_id={"sample": other}, device_id_type=MESH)

    w128[...] = jnp.zeros_like(w128)
    get_wout.wait()
    w128[:, 0:fields] = wout_v[...]
    get_win.wait()

    def remote(src, dst, ss, rs, axis, index):
        return pltpu.make_async_remote_copy(
            src_ref=src, dst_ref=dst, send_sem=ss, recv_sem=rs,
            device_id={axis: index}, device_id_type=MESH,
        )

    f_copies = []
    for i in range(MZ):
        base = rows_of(i)
        get_x[i].wait()
        pre[pl.ds(base, step)] = jnp.dot(
            x_v[pl.ds(base, step)], win_v[...], preferred_element_type=F32
        )

        @pl.loop(0, step // 16)
        def _(n):
            at = pl.ds(pl.multiple_of(base + n * 16, 16), 16)
            z = pre[at] + bin_ref[...]
            pre[at] = z
            t = jnp.tanh(z * (GELU_C + (GELU_C * GELU_A) * (z * z)))
            hz = 0.5 * z
            act[at] = (hz + hz * t).astype(BF16)

        value = jnp.dot(act[pl.ds(base, step)], w128[...], preferred_element_type=F32)
        zq = lax.rem(mz + 1 + i, MZ)
        fsend[pl.ds(zq * MX, MX)] = value.reshape(MX, per, LANES).astype(BF16)
        if i == 0:
            pl.semaphore_wait(barrier, (M - 1) + (G - 1) + 1)
        for o in range(MX):
            if i == MZ - 1 and o == 0:
                continue
            j = zq * MX + lax.rem(mx + o, MX)
            copy = remote(
                fsend.at[j], frecv.at[me], f_ss.at[i * MX + o], f_rs.at[i * MX + o], "member", j
            )
            copy.start()
            f_copies.append(copy)
    frecv[pl.ds(me, 1)] = fsend[pl.ds(me, 1)]

    get_t.wait()
    t128[...] = jnp.zeros_like(t128)
    t128[0:fields] = tv[...]
    t128[fields : fields + 1] = area_ref[...]
    tt[...] = t128[...].T
    bout = jnp.concatenate([bout_ref[...], jnp.zeros((1, LANES - fields), F32)], axis=1)
    var = jnp.concatenate([var_ref[...], jnp.zeros((1, LANES - fields), F32)], axis=1)
    eps_fair = (1.0 - alpha_fair) / M
    pairwise = (1.0 - eps_fair) / (M * (M - 1))
    loss_scale = M / math.sqrt(S * G * points)

    for copy in f_copies:
        copy.wait_recv()

    @pl.loop(0, per // 16)
    def _(n):
        at = pl.ds(pl.multiple_of(n * 16, 16), 16)
        seen = tt[pl.ds(pl.multiple_of(me * per + n * 16, 16), 16)]
        scale = (loss_scale * seen[:, fields : fields + 1]) * var
        target = seen - bout
        f = [frecv[j, at].astype(F32) for j in range(M)]
        total = [jnp.zeros((16, LANES), F32) for _ in range(M)]
        for j in range(M):
            for k in range(j + 1, M):
                slope = softened_slope(f[j] - f[k])
                total[j] = total[j] + slope
                total[k] = total[k] - slope
        for j in range(M):
            g = scale * (softened_slope(f[j] - target) * (1.0 / M) - pairwise * total[j])
            gsend[j, at] = g.astype(BF16)

    g_copies = {}
    for i in (1, 2, 0, 3):
        zq = lax.rem(mz + 1 + i, MZ)
        for o in range(MX):
            if i == MZ - 1 and o == 0:
                continue
            j = zq * MX + lax.rem(mx + o, MX)
            copy = remote(
                gsend.at[j], grecv.at[me], g_ss.at[i * MX + o], g_rs.at[i * MX + o], "member", j
            )
            copy.start()
            g_copies[(i, o)] = copy
    grecv[pl.ds(me, 1)] = gsend[pl.ds(me, 1)]

    @pl.loop(0, points // 16)
    def _(n):
        at = pl.ds(pl.multiple_of(n * 16, 16), 16)
        z = pre[at]
        q = z * z
        t = jnp.tanh(z * (GELU_C + (GELU_C * GELU_A) * q))
        inner = GELU_C + (3.0 * GELU_C * GELU_A) * q
        pre[at] = (0.5 + 0.5 * t) + (0.5 * z) * (1.0 - t * t) * inner

    w128t[...] = w128[...].T
    for n in range(points // 256):
        xt_v[:, n * 256 : (n + 1) * 256] = x_v[n * 256 : (n + 1) * 256, :].T
    bias_acc[...] = jnp.zeros_like(bias_acc)

    for i in (3, 0, 2, 1):
        for o in range(MX):
            if (i, o) in g_copies:
                g_copies[(i, o)].wait_recv()
        zq = lax.rem(mz + 2 * MZ - 1 - i, MZ)
        base = pl.multiple_of(zq * step, step)
        rows = grecv[pl.ds(zq * MX, MX)].reshape(step, LANES)
        back = jnp.dot(rows, w128t[...], preferred_element_type=F32)
        pre[pl.ds(base, step)] = pre[pl.ds(base, step)] * back

        @pl.loop(0, step // 16)
        def _(n):
            at = pl.ds(pl.multiple_of(base + n * 16, 16), 16)
            value = pre[at]
            pg[at] = value.astype(BF16)
            bias_acc[...] += value[0:8] + value[8:16]

    goutt[...] = lax.dot_general(
        grecv[...].reshape(points, LANES), act[...], (((0,), (0,)), ((), ())),
        preferred_element_type=F32,
    )
    goutt[fields : fields + 1] = jnp.sum(bias_acc[...], axis=0, keepdims=True)
    chunks = half // LANES
    blocks = (G, MZ, MX, R, LANES)
    last = chunks
    kind = csend.dtype
    csend[last] = goutt[...].T.reshape(blocks).astype(kind)

    c_copies = []

    def exchange(n):
        copy = remote(csend.at[n], crecv.at[n], c_ss.at[n], c_rs.at[n], "sample", other)
        copy.start()
        c_copies.append(copy)

    exchange(last)
    per_dot = 2
    wide = per_dot * LANES
    for n in range(0, chunks, per_dot):
        at = pl.ds(pl.multiple_of(other * half + n * LANES, LANES), wide)
        value = jnp.dot(xt_v[...], pg[:, at], preferred_element_type=F32)
        for u in range(per_dot):
            csend[n + u] = value[:, u * LANES : (u + 1) * LANES].reshape(blocks).astype(kind)
            exchange(n + u)

    lengths = {"x": MX, "y": G, "z": MZ}
    index = {"x": mx, "y": grid, "z": mz}
    sem_base = {}
    sem_count = 0
    for n in range(chunks + 1):
        for stage in range(3):
            sem_base[(n, stage)] = sem_count
            sem_count += lengths[chunk_axes[n][stage]] - 1
    live = {}

    def peer(axis, to):
        if axis == "y":
            return "grid", to
        if axis == "x":
            return "member", mz * MX + to
        return "member", to * MX + mx

    def part(ref, axes, axis, to):
        where = [slice(None)] * len(axes)
        where[axes.index(axis)] = to
        return ref.at[tuple(where)]

    def send(n, stage, src, dst, axes):
        axis = chunk_axes[n][stage]
        started = []
        for s in range(1, lengths[axis]):
            to = lax.rem(index[axis] + s, lengths[axis])
            name, where = peer(axis, to)
            sem = sem_base[(n, stage)] + s - 1
            copy = remote(
                part(src, axes, axis, to), dst.at[s - 1], r_ss.at[sem], r_rs.at[sem], name, where
            )
            copy.start()
            started.append(copy)
        live[(n, stage)] = started

    def first(n):
        c_copies_of[n].wait_recv()
        if n == last:
            total = csend[n].astype(F32) + crecv[n].astype(F32)
        else:
            total = own[n] + crecv[n].astype(F32)
            own[n] = total
        s1[n] = total.astype(kind)
        send(n, 0, s1.at[n], r1[n], "yzx")

    def arrived(n, stage, kept, source):
        total = kept
        for s, copy in enumerate(live[(n, stage)]):
            copy.wait_recv()
            total = total + source[s].astype(F32)
        return total

    def second(n):
        axis = chunk_axes[n][0]
        source = s1.at[n] if n == last else own.at[n]
        kept = part(source, "yzx", axis, index[axis])[...].astype(F32)
        total = arrived(n, 0, kept, r1[n])
        acc[0][n][...] = total
        s2[n][...] = total.astype(kind)
        send(n, 1, s2[n], r2[n], "yzx".replace(axis, ""))

    def third(n):
        axes = "yzx".replace(chunk_axes[n][0], "")
        axis = chunk_axes[n][1]
        kept = part(acc[0][n], axes, axis, index[axis])[...]
        total = arrived(n, 1, kept, r2[n])
        acc[1][n][...] = total
        s3[n][...] = total.astype(kind)
        send(n, 2, s3[n], r3[n], axes.replace(axis, ""))

    e_copies = []

    def finish(n):
        axis = chunk_axes[n][2]
        total = arrived(n, 2, acc[1][n][index[axis]], r3[n])
        if n == last:
            gout_ref[...] = total[:, 0:fields]
            gbias_ref[...] = total.T[fields : fields + 1, :]
            return
        fin_s[n] = total
        copy = remote(fin_s.at[n], fin_r.at[n], e_ss.at[n], e_rs.at[n], "sample", other)
        copy.start()
        e_copies.append(copy)
        at = pl.ds(pl.multiple_of(core * half + n * LANES, LANES), LANES)
        gin_ref[:, at] = total

    c_copies_of = dict(zip([last] + list(range(chunks)), c_copies))
    first(last)
    for n in range(0, chunks, per_dot):
        at = pl.ds(pl.multiple_of(core * half + n * LANES, LANES), wide)
        value = jnp.dot(xt_v[...], pg[:, at], preferred_element_type=F32)
        for u in range(per_dot):
            own[n + u] = value[:, u * LANES : (u + 1) * LANES].reshape(blocks)
            first(n + u)
    order = [last] + list(range(chunks))
    plan = []
    for place, n in enumerate(order):
        plan.append((place, 0, second, n))
        plan.append((place + 2, 1, third, n))
        plan.append((place + 4, 2, finish, n))
    plan.sort(key=lambda entry: entry[:2])
    for _, _, act_on, n in plan:
        act_on(n)
    for n in range(chunks):
        e_copies[n].wait_recv()
        at = pl.ds(pl.multiple_of(other * half + n * LANES, LANES), LANES)
        gin_ref[:, at] = fin_r[n]

    for copy in f_copies + list(g_copies.values()) + c_copies + e_copies:
        copy.wait_send()
    for started in live.values():
        for copy in started:
            copy.wait_send()


def local(
    sizes, hidden_states, targets, area_weight, var_weight, weight_in, bias_in, output_weight,
    output_bias,
):
    G, M, S = sizes
    MZ = MEMBER_ROWS
    MX = M // MZ
    points, depth = hidden_states.shape[2:]
    width, fields = output_weight.shape
    R = width // (G * M)
    per = points // M
    kind = BF16 if R % 16 == 0 else F32
    chunks = width // S // LANES
    chunk_axes = [ORDERS[n % 4] for n in range(chunks)] + [ORDERS[4]]
    lengths = {"x": MX, "y": G, "z": MZ}

    def dims(axes):
        return tuple(lengths[a] for a in axes)

    r1, s2, r2, a2, s3, r3, a3 = [], [], [], [], [], [], []
    sems = 0
    for axes in chunk_axes:
        rest = "yzx".replace(axes[0], "")
        one = rest.replace(axes[1], "")
        r1.append(pltpu.VMEM((lengths[axes[0]] - 1, *dims(rest), R, LANES), kind))
        s2.append(pltpu.VMEM((*dims(rest), R, LANES), kind))
        a2.append(pltpu.VMEM((*dims(rest), R, LANES), F32))
        r2.append(pltpu.VMEM((lengths[axes[1]] - 1, *dims(one), R, LANES), kind))
        s3.append(pltpu.VMEM((*dims(one), R, LANES), kind))
        a3.append(pltpu.VMEM((*dims(one), R, LANES), F32))
        r3.append(pltpu.VMEM((lengths[axes[2]] - 1, R, LANES), kind))
        sems += sum(lengths[a] - 1 for a in axes)
    blocks = (G, MZ, MX, R, LANES)
    dma = pltpu.SemaphoreType.DMA
    scratch = [
        pltpu.VMEM((points, depth), BF16),
        pltpu.VMEM((depth, points), BF16),
        pltpu.VMEM((depth, width), BF16),
        pltpu.VMEM((width, fields), BF16),
        pltpu.VMEM((width, LANES), BF16),
        pltpu.VMEM((LANES, width), BF16),
        pltpu.VMEM((fields, points), F32),
        pltpu.VMEM((LANES, points), F32),
        pltpu.VMEM((points, LANES), F32),
        pltpu.VMEM((points, width), F32),
        pltpu.VMEM((points, width), BF16),
        pltpu.VMEM((points, width), BF16),
        pltpu.VMEM((8, width), F32),
        pltpu.VMEM((M, per, LANES), BF16),
        pltpu.VMEM((M, per, LANES), BF16),
        pltpu.VMEM((M, per, LANES), BF16),
        pltpu.VMEM((M, per, LANES), BF16),
        pltpu.VMEM((LANES, width), F32),
        pltpu.VMEM((chunks + 1, *blocks), kind),
        pltpu.VMEM((chunks + 1, *blocks), kind),
        pltpu.VMEM((chunks, *blocks), F32),
        pltpu.VMEM((chunks + 1, *blocks), kind),
        r1, s2, r2, s3, r3, [a2, a3],
        pltpu.VMEM((chunks, R, LANES), F32),
        pltpu.VMEM((chunks, R, LANES), F32),
        dma((3 + MZ,)), dma((M,)), dma((M,)), dma((M,)), dma((M,)),
        dma((chunks + 1,)), dma((chunks + 1,)), dma((sems,)), dma((sems,)),
        dma((chunks,)), dma((chunks,)),
    ]
    flat, tree = jax.tree.flatten(scratch, is_leaf=lambda leaf: not isinstance(leaf, list))

    def body(*refs):
        head, tail = refs[:11], refs[11:]
        kernel(
            (G, MZ, MX, S, R), chunk_axes, *head, *jax.tree.unflatten(tree, tail)
        )

    whole = pl.BlockSpec(memory_space=pltpu.VMEM)
    anywhere = pl.BlockSpec(memory_space=pl.ANY)
    flops = 4 * points * depth * width + 6 * points * width * LANES
    gin, gbias, gout = pl.pallas_call(
        body,
        out_shape=(
            jax.ShapeDtypeStruct((R, width), F32),
            jax.ShapeDtypeStruct((1, R), F32),
            jax.ShapeDtypeStruct((R, fields), F32),
        ),
        in_specs=[anywhere, anywhere, whole, whole, anywhere, whole, anywhere, whole],
        out_specs=(whole, whole, whole),
        scratch_shapes=flat,
        compiler_params=pltpu.CompilerParams(
            collective_id=0, has_side_effects=True, vmem_limit_bytes=56 * 1024 * 1024
        ),
        cost_estimate=pl.CostEstimate(
            flops=flops, bytes_accessed=6 * 1024 * 1024, transcendentals=2 * points * width
        ),
        name="crps_gradient",
    )(
        hidden_states, targets, area_weight[None], var_weight[None], weight_in, bias_in[None],
        output_weight, output_bias[None],
    )
    return gin, gbias.reshape(R), gout


def solution(mesh):
    placed = (
        P("sample", "member", "grid", None),
        P("sample", None, "grid"),
        P("grid"),
        P(),
        P(),
        P(),
        P(),
        P(),
    )
    sizes = (mesh.shape["grid"], mesh.shape["member"], mesh.shape["sample"])
    return jax.shard_map(
        functools.partial(local, sizes),
        mesh=mesh,
        in_specs=placed,
        out_specs=(P(("grid", "member"), None), P(("grid", "member")), P(("grid", "member"), None)),
        check_vma=False,
    )
```

```python
import functools
import math

import jax
import jax.numpy as jnp
from jax import lax
from jax.experimental import pallas as pl
from jax.experimental.pallas import tpu as pltpu
from jax.sharding import PartitionSpec as P

smoothing = 0.01
alpha_fair = 0.95
LANES = 128
MEMBER_ROWS = 4
GELU_C = math.sqrt(2.0 / math.pi)
GELU_A = 0.044715
MESH = pl.DeviceIdType.MESH
F32 = jnp.float32
BF16 = jnp.bfloat16
ORDERS = ("xzy", "yzx", "xyz", "yxz", "zxy")
PLAN = ((0, 0), (0, 1), (0, 4), (0, 2), (0, 3), (1, 0), (1, 1), (1, 4), (1, 2), (1, 3))


def softened_slope(value):
    return value * lax.rsqrt(value * value + smoothing)


def kernel(
    sizes, chunk_axes,
    x_hbm, t_hbm, area_ref, var_ref, win_hbm, bin_ref, wout_hbm, bout_ref,
    gin_ref, gbias_ref, gout_ref,
    x_v, xt_v, win_v, wout_v, w128, w128t, tv, tt,
    pre, act, pg, bias_acc, fsend, frecv, gsend, grecv, goutt,
    csend, crecv, own, o_all, o_fin, s1, r1, s2, r2, s3, r3, acc, fin_s, fin_r,
    in_sem, f_ss, f_rs, g_ss, g_rs, c_ss, c_rs, r_ss, r_rs, e_ss, e_rs,
):
    G, MZ, MX, S, R = sizes
    M = MZ * MX
    points, depth = x_v.shape
    width = win_v.shape[1]
    fields = wout_v.shape[0]
    tiles = tv.shape[0]
    per = points // M
    step = points // MZ
    half = width // S
    grid = lax.axis_index("grid")
    me = lax.axis_index("member")
    core = lax.axis_index("sample")
    mz, mx = me // MX, me % MX
    other = 1 - core

    pending = []

    def fetch(src, dst, n):
        copy = pltpu.make_async_copy(src, dst, in_sem.at[n])
        copy.start()
        return copy

    def rows_of(i):
        return pl.multiple_of(lax.rem(mz + 1 + i, MZ) * step, step)

    get_win = fetch(win_hbm, win_v, 0)
    get_x = [
        fetch(x_hbm.at[0, 0, pl.ds(rows_of(i), step)], x_v.at[pl.ds(rows_of(i), step)], 1 + i)
        for i in range(MZ)
    ]
    get_wout = fetch(wout_hbm, wout_v, 1 + MZ)
    tile = (me * per) // LANES
    get_t = [fetch(t_hbm.at[:, tile + n], tv.at[n], 2 + MZ + n) for n in range(tiles)]

    barrier = pltpu.get_barrier_semaphore()
    for s in range(1, M):
        pl.semaphore_signal(barrier, inc=1, device_id={"member": lax.rem(me + s, M)}, device_id_type=MESH)
    for s in range(1, G):
        pl.semaphore_signal(barrier, inc=1, device_id={"grid": lax.rem(grid + s, G)}, device_id_type=MESH)
    pl.semaphore_signal(barrier, inc=1, device_id={"sample": other}, device_id_type=MESH)

    w128t[...] = jnp.zeros_like(w128t)
    get_wout.wait()
    w128t[0:fields] = wout_v[...]
    w128[...] = w128t[...].T
    get_win.wait()

    def remote(src, dst, ss, rs, axis, index):
        return pltpu.make_async_remote_copy(
            src_ref=src, dst_ref=dst, send_sem=ss, recv_sem=rs,
            device_id={axis: index}, device_id_type=MESH,
        )

    f_copies = []
    for i in range(MZ):
        base = rows_of(i)
        get_x[i].wait()
        pre[pl.ds(base, step)] = jnp.dot(
            x_v[pl.ds(base, step)], win_v[...], preferred_element_type=F32
        )

        @pl.loop(0, step // 16)
        def _(n):
            at = pl.ds(pl.multiple_of(base + n * 16, 16), 16)
            z = pre[at] + bin_ref[...]
            pre[at] = z
            t = jnp.tanh(z * (GELU_C + (GELU_C * GELU_A) * (z * z)))
            hz = 0.5 * z
            act[at] = (hz + hz * t).astype(BF16)

        value = jnp.dot(act[pl.ds(base, step)], w128[...], preferred_element_type=F32)
        zq = lax.rem(mz + 1 + i, MZ)
        fsend[pl.ds(zq * MX, MX)] = value.reshape(MX, per, LANES).astype(BF16)
        if i == 0:
            pl.semaphore_wait(barrier, (M - 1) + (G - 1) + 1)
        for o in range(MX):
            if i == MZ - 1 and o == 0:
                continue
            j = zq * MX + lax.rem(mx + o, MX)
            copy = remote(
                fsend.at[j], frecv.at[me], f_ss.at[i * MX + o], f_rs.at[i * MX + o], "member", j
            )
            copy.start()
            f_copies.append(copy)
    frecv[pl.ds(me, 1)] = fsend[pl.ds(me, 1)]

    for n in range(tiles):
        get_t[n].wait()
        rest = jnp.zeros((LANES - fields - 1, LANES), F32)
        tt[n * LANES : (n + 1) * LANES] = jnp.concatenate(
            [tv[n], area_ref[pl.ds(tile + n, 1)], rest], axis=0
        ).T
    shift = me * per - tile * LANES
    bout = jnp.concatenate([bout_ref[...], jnp.zeros((1, LANES - fields), F32)], axis=1)
    var = jnp.concatenate([var_ref[...], jnp.zeros((1, LANES - fields), F32)], axis=1)
    eps_fair = (1.0 - alpha_fair) / M
    pairwise = (1.0 - eps_fair) / (M * (M - 1))
    loss_scale = M / math.sqrt(S * G * points)

    for copy in f_copies:
        copy.wait_recv()

    @pl.loop(0, per // 16)
    def _(n):
        at = pl.ds(pl.multiple_of(n * 16, 16), 16)
        seen = tt[pl.ds(pl.multiple_of(shift + n * 16, 16), 16)]
        scale = (loss_scale * seen[:, fields : fields + 1]) * var
        target = seen - bout
        f = [frecv[j, at].astype(F32) for j in range(M)]
        total = [jnp.zeros((16, LANES), F32) for _ in range(M)]
        for j in range(M):
            for k in range(j + 1, M):
                slope = softened_slope(f[j] - f[k])
                total[j] = total[j] + slope
                total[k] = total[k] - slope
        for j in range(M):
            g = scale * (softened_slope(f[j] - target) * (1.0 / M) - pairwise * total[j])
            gsend[j, at] = g.astype(BF16)

    g_copies = {}
    for i in (1, 2, 0, 3):
        zq = lax.rem(mz + 1 + i, MZ)
        for o in range(MX):
            if i == MZ - 1 and o == 0:
                continue
            j = zq * MX + lax.rem(mx + o, MX)
            copy = remote(
                gsend.at[j], grecv.at[me], g_ss.at[i * MX + o], g_rs.at[i * MX + o], "member", j
            )
            copy.start()
            g_copies[(i, o)] = copy
    grecv[pl.ds(me, 1)] = gsend[pl.ds(me, 1)]

    @pl.loop(0, points // 16)
    def _(n):
        at = pl.ds(pl.multiple_of(n * 16, 16), 16)
        z = pre[at]
        q = z * z
        t = jnp.tanh(z * (GELU_C + (GELU_C * GELU_A) * q))
        inner = GELU_C + (3.0 * GELU_C * GELU_A) * q
        pre[at] = (0.5 + 0.5 * t) + (0.5 * z) * (1.0 - t * t) * inner

    for n in range(points // 256):
        xt_v[:, n * 256 : (n + 1) * 256] = x_v[n * 256 : (n + 1) * 256, :].T
    bias_acc[...] = jnp.zeros_like(bias_acc)

    for i in (3, 0, 2, 1):
        for o in range(MX):
            if (i, o) in g_copies:
                g_copies[(i, o)].wait_recv()
        zq = lax.rem(mz + 2 * MZ - 1 - i, MZ)
        base = pl.multiple_of(zq * step, step)
        rows = grecv[pl.ds(zq * MX, MX)].reshape(step, LANES)
        back = jnp.dot(rows, w128t[...], preferred_element_type=F32)
        pre[pl.ds(base, step)] = pre[pl.ds(base, step)] * back

        @pl.loop(0, step // 16)
        def _(n):
            at = pl.ds(pl.multiple_of(base + n * 16, 16), 16)
            value = pre[at]
            pg[at] = value.astype(BF16)
            bias_acc[...] += value[0:8] + value[8:16]

    goutt[...] = lax.dot_general(
        grecv[...].reshape(points, LANES), act[...], (((0,), (0,)), ((), ())),
        preferred_element_type=F32,
    )
    goutt[fields : fields + 1] = jnp.sum(bias_acc[...], axis=0, keepdims=True)
    chunks = half // LANES
    last = chunks
    kind = s1[0].dtype
    split = o_fin.shape[1] < R
    blocks = (G, MZ, MX, R, LANES)
    o_all[...] = goutt[...].T.reshape(o_all.shape)
    lengths = {"x": MX, "y": G, "z": MZ}
    index = {"x": mx, "y": grid, "z": mz}
    sem_base = {}
    sem_count = 0
    for n in range(chunks + 1):
        for stage in range(3):
            sem_base[(n, stage)] = sem_count
            sem_count += lengths[chunk_axes[n][stage]] - 1
    live = {}

    def peer(axis, to):
        if axis == "y":
            return "grid", to
        if axis == "x":
            return "member", mz * MX + to
        return "member", to * MX + mx

    def part(ref, axes, axis, to):
        where = [slice(None)] * len(axes)
        where[axes.index(axis)] = to
        return ref.at[tuple(where)]

    def send(n, stage, src, dst, axes):
        axis = chunk_axes[n][stage]
        started = []
        for s in range(1, lengths[axis]):
            to = lax.rem(index[axis] + s, lengths[axis])
            name, where = peer(axis, to)
            sem = sem_base[(n, stage)] + s - 1
            copy = remote(
                part(src, axes, axis, to), dst.at[s - 1], r_ss.at[sem], r_rs.at[sem], name, where
            )
            copy.start()
            started.append(copy)
        live[(n, stage)] = started

    c_copies = {}

    def exchange(n):
        copy = remote(csend[n], crecv[n], c_ss.at[n], c_rs.at[n], "sample", other)
        copy.start()
        c_copies[n] = copy

    def columns(n, owner):
        at = pl.ds(pl.multiple_of(owner * half + n * LANES, LANES), 2 * LANES)
        value = jnp.dot(xt_v[...], pg[:, at], preferred_element_type=F32)
        return [value[:, u * LANES : (u + 1) * LANES].reshape(blocks) for u in range(2)]

    def give(n):
        for u, value in enumerate(columns(n, other)):
            csend[n + u][...] = value.astype(kind)
            exchange(n + u)

    def keep(n):
        for u, value in enumerate(columns(n, core)):
            own[n + u][...] = value

    def first(n):
        c_copies[n].wait_recv()
        total = own[n][...] + crecv[n][...].astype(F32)
        own[n][...] = total
        s1[n][...] = total.astype(kind)
        send(n, 0, s1[n], r1[n], "yzx")

    def arrived(n, stage, kept, source):
        total = kept
        for s, copy in enumerate(live[(n, stage)]):
            copy.wait_recv()
            total = total + source[s].astype(F32)
        return total

    def second(n):
        axis = chunk_axes[n][0]
        kept = part(own[n], "yzx", axis, index[axis])[...]
        total = arrived(n, 0, kept, r1[n])
        acc[0][n][...] = total
        s2[n][...] = total.astype(kind)
        send(n, 1, s2[n], r2[n], "yzx".replace(axis, ""))

    def third(n):
        axes = "yzx".replace(chunk_axes[n][0], "")
        axis = chunk_axes[n][1]
        kept = part(acc[0][n], axes, axis, index[axis])[...]
        total = arrived(n, 1, kept, r2[n])
        acc[1][n][...] = total
        s3[n][...] = total.astype(kind)
        send(n, 2, s3[n], r3[n], axes.replace(axis, ""))

    e_copies = {}

    def finish(n):
        axis = chunk_axes[n][2]
        total = arrived(n, 2, acc[1][n][index[axis]], r3[n])
        if n == last:
            o_fin[core if split else 0] = total
            if not split:
                return
        else:
            at = pl.ds(pl.multiple_of(core * half + n * LANES, LANES), LANES)
            gin_ref[:, at] = total
        fin_s[n][...] = total
        copy = remote(fin_s[n], fin_r[n], e_ss.at[n], e_rs.at[n], "sample", other)
        copy.start()
        e_copies[n] = copy

    left = set()

    def gone(n, stage):
        for copy in live[(n, stage)]:
            copy.wait_send()
        left.add((n, stage))

    give(0)
    if split:
        csend[last][...] = o_all[:, :, :, other].astype(kind)
        own[last][...] = o_all[:, :, :, core]
    else:
        csend[last][...] = o_all[:, :, :, 0].astype(kind)
        own[last][...] = csend[last][...].astype(F32)
    exchange(last)
    keep(0)
    for n in (0, 1, last):
        first(n)
    for n in range(2, chunks, 2):
        give(n)
        keep(n)
    for n in range(2, chunks):
        gone(n - 2, 0)
        first(n)
    for stage, n in PLAN:
        (second, third)[stage](n)
    for n in (last, *range(chunks)):
        finish(n)
    for n in range(chunks):
        e_copies[n].wait_recv()
        at = pl.ds(pl.multiple_of(other * half + n * LANES, LANES), LANES)
        gin_ref[:, at] = fin_r[n][...]
    if split:
        e_copies[last].wait_recv()
        o_fin[other] = fin_r[last][...]
    total = o_fin[...].reshape(R, LANES)
    gout_ref[...] = total[:, 0:fields]
    gbias_ref[...] = total.T[fields : fields + 1, :]

    for copies in (g_copies, c_copies, e_copies):
        f_copies = f_copies + list(copies.values())
    for copy in f_copies:
        copy.wait_send()
    for key in live:
        if key not in left:
            gone(*key)


def hand_over(gin_ref, gbias_ref, gout_ref, gin_out, gbias_out, gout_out):
    gin_out[...] = gin_ref[...]
    gbias_out[...] = gbias_ref[...]
    gout_out[...] = gout_ref[...]


def local(
    sizes, hidden_states, targets, area_weight, var_weight, weight_in, bias_in, output_weight,
    output_bias,
):
    G, M, S = sizes
    MZ = MEMBER_ROWS
    MX = M // MZ
    points, depth = hidden_states.shape[2:]
    width, fields = output_weight.shape
    R = width // (G * M)
    per = points // M
    tiles = max(1, per // LANES)
    kind = BF16 if R % 16 == 0 else F32
    chunks = width // S // LANES
    chunk_axes = [ORDERS[n % 4] for n in range(chunks)] + [ORDERS[4]]
    lengths = {"x": MX, "y": G, "z": MZ}

    def dims(axes):
        return tuple(lengths[a] for a in axes)

    s1, r1, s2, r2, a2, s3, r3, a3, f32_own, fin = [], [], [], [], [], [], [], [], [], []
    sems = 0
    split = S == 2 and R % 32 == 0
    for n, axes in enumerate(chunk_axes):
        rows = R // 2 if split and n == chunks else R
        rest = "yzx".replace(axes[0], "")
        one = rest.replace(axes[1], "")
        tile = (rows, LANES)
        s1.append(pltpu.VMEM((*dims("yzx"), *tile), kind))
        f32_own.append(pltpu.VMEM((*dims("yzx"), *tile), F32))
        r1.append(pltpu.VMEM((lengths[axes[0]] - 1, *dims(rest), *tile), kind))
        s2.append(pltpu.VMEM((*dims(rest), *tile), kind))
        a2.append(pltpu.VMEM((*dims(rest), *tile), F32))
        r2.append(pltpu.VMEM((lengths[axes[1]] - 1, *dims(one), *tile), kind))
        s3.append(pltpu.VMEM((*dims(one), *tile), kind))
        a3.append(pltpu.VMEM((*dims(one), *tile), F32))
        r3.append(pltpu.VMEM((lengths[axes[2]] - 1, *tile), kind))
        fin.append(pltpu.VMEM(tile, F32))
        sems += sum(lengths[a] - 1 for a in axes)
    halves = 2 if split else 1
    o_all = pltpu.VMEM((G, MZ, MX, halves, R // halves, LANES), F32)
    o_fin = pltpu.VMEM((halves, R // halves, LANES), F32)
    dma = pltpu.SemaphoreType.DMA
    scratch = [
        pltpu.VMEM((points, depth), BF16),
        pltpu.VMEM((depth, points), BF16),
        pltpu.VMEM((depth, width), BF16),
        pltpu.VMEM((fields, width), BF16),
        pltpu.VMEM((width, LANES), BF16),
        pltpu.VMEM((LANES, width), BF16),
        pltpu.VMEM((tiles, fields, LANES), F32),
        pltpu.VMEM((tiles * LANES, LANES), F32),
        pltpu.VMEM((points, width), F32),
        pltpu.VMEM((points, width), BF16),
        pltpu.VMEM((points, width), BF16),
        pltpu.VMEM((8, width), F32),
        pltpu.VMEM((M, per, LANES), BF16),
        pltpu.VMEM((M, per, LANES), BF16),
        pltpu.VMEM((M, per, LANES), BF16),
        pltpu.VMEM((M, per, LANES), BF16),
        pltpu.VMEM((LANES, width), F32),
        s1, s1, f32_own, o_all, o_fin, s1, r1, s2, r2, s3, r3, [a2, a3], fin, fin,
        dma((2 + MZ + tiles,)), dma((M,)), dma((M,)), dma((M,)), dma((M,)),
        dma((chunks + 1,)), dma((chunks + 1,)), dma((sems,)), dma((sems,)),
        dma((chunks + 1,)), dma((chunks + 1,)),
    ]
    flat, tree = jax.tree.flatten(scratch, is_leaf=lambda leaf: not isinstance(leaf, list))

    def body(*refs):
        head, tail = refs[:11], refs[11:]
        kernel(
            (G, MZ, MX, S, R), chunk_axes, *head, *jax.tree.unflatten(tree, tail)
        )

    whole = pl.BlockSpec(memory_space=pltpu.VMEM)
    anywhere = pl.BlockSpec(memory_space=pl.ANY)
    flops = 4 * points * depth * width + 6 * points * width * LANES
    gin, gbias, gout = pl.pallas_call(
        body,
        out_shape=(
            jax.ShapeDtypeStruct((R, width), F32),
            jax.ShapeDtypeStruct((1, R), F32),
            jax.ShapeDtypeStruct((R, fields), F32),
        ),
        in_specs=[anywhere, anywhere, whole, whole, anywhere, whole, anywhere, whole],
        out_specs=(whole, whole, whole),
        scratch_shapes=flat,
        compiler_params=pltpu.CompilerParams(
            collective_id=0, has_side_effects=True, vmem_limit_bytes=56 * 1024 * 1024
        ),
        cost_estimate=pl.CostEstimate(
            flops=flops, bytes_accessed=6 * 1024 * 1024, transcendentals=2 * points * width
        ),
        name="crps_gradient",
    )(
        hidden_states, targets.reshape(fields, points // LANES, LANES),
        area_weight.reshape(points // LANES, LANES), var_weight[None], weight_in, bias_in[None],
        output_weight.T, output_bias[None],
    )
    gin, gbias, gout = pl.pallas_call(
        hand_over,
        out_shape=(
            jax.ShapeDtypeStruct((R, width), F32),
            jax.ShapeDtypeStruct((1, R), F32),
            jax.ShapeDtypeStruct((R, fields), F32),
        ),
        in_specs=[whole, whole, whole],
        out_specs=(whole, whole, whole),
        name="results",
    )(gin, gbias, gout)
    return gin, gbias.reshape(R), gout


def solution(mesh):
    placed = (
        P("sample", "member", "grid", None),
        P("sample", None, "grid"),
        P("grid"),
        P(),
        P(),
        P(),
        P(),
        P(),
    )
    sizes = (mesh.shape["grid"], mesh.shape["member"], mesh.shape["sample"])
    return jax.shard_map(
        functools.partial(local, sizes),
        mesh=mesh,
        in_specs=placed,
        out_specs=(P(("grid", "member"), None), P(("grid", "member")), P(("grid", "member"), None)),
        check_vma=False,
    )
```

```python
import functools
import math

import jax
import jax.numpy as jnp
from jax import lax
from jax.experimental import pallas as pl
from jax.experimental.pallas import tpu as pltpu
from jax.sharding import PartitionSpec as P

smoothing = 0.01
alpha_fair = 0.95
LANES = 128
MEMBER_ROWS = 4
GELU_C = math.sqrt(2.0 / math.pi)
GELU_A = 0.044715
MESH = pl.DeviceIdType.MESH
F32 = jnp.float32
BF16 = jnp.bfloat16
ORDERS = ("xzy", "yzx", "xyz", "yxz", "zxy")
PLAN = ((0, 0), (0, 1), (0, 4), (0, 2), (0, 3), (1, 0), (1, 1), (1, 4), (1, 2), (1, 3))


def softened_slope(value):
    return value * lax.rsqrt(value * value + smoothing)


def kernel(
    sizes, chunk_axes,
    x_hbm, t_hbm, area_ref, var_ref, win_hbm, bin_ref, wout_hbm, bout_ref,
    gin_ref, gbias_ref, gout_ref,
    x_v, xt_v, win_v, wout_v, w128, w128t, tv, tt,
    pre, act, pg, bias_acc, fsend, frecv, gsend, grecv, goutt,
    csend, crecv, own, o_all, o_fin, s1, r1, s2, r2, s3, r3, acc, fin_s, fin_r,
    in_sem, f_ss, f_rs, g_ss, g_rs, c_ss, c_rs, r_ss, r_rs, e_ss, e_rs,
):
    G, MZ, MX, S, R = sizes
    M = MZ * MX
    waves, _, pw, depth = x_v.shape
    points = waves * M * pw
    width = win_v.shape[1]
    fields = wout_v.shape[0]
    tiles = tv.shape[0]
    per = points // M
    step = M * pw
    half = width // S
    grid = lax.axis_index("grid")
    me = lax.axis_index("member")
    core = lax.axis_index("sample")
    mz, mx = me // MX, me % MX
    other = 1 - core

    pending = []

    def fetch(src, dst, n):
        copy = pltpu.make_async_copy(src, dst, in_sem.at[n])
        copy.start()
        return copy

    def fetch_x(w):
        return fetch(x_hbm.at[:, w], x_v.at[w], 1 + w)

    get_x = [fetch_x(0)]
    get_win = fetch(win_hbm, win_v, 0)
    get_wout = fetch(wout_hbm, wout_v, 1 + waves)
    tile = (me * per) // LANES

    barrier = pltpu.get_barrier_semaphore()
    for s in range(1, M):
        pl.semaphore_signal(barrier, inc=1, device_id={"member": lax.rem(me + s, M)}, device_id_type=MESH)
    for s in range(1, G):
        pl.semaphore_signal(barrier, inc=1, device_id={"grid": lax.rem(grid + s, G)}, device_id_type=MESH)
    pl.semaphore_signal(barrier, inc=1, device_id={"sample": other}, device_id_type=MESH)

    w128t[...] = jnp.zeros_like(w128t)
    get_wout.wait()
    w128t[0:fields] = wout_v[...]
    w128[...] = w128t[...].T
    get_win.wait()
    get_x += [fetch_x(w) for w in range(1, waves)]
    get_t = [fetch(t_hbm.at[:, tile + n], tv.at[n], 2 + waves + n) for n in range(tiles)]

    def remote(src, dst, ss, rs, axis, index):
        return pltpu.make_async_remote_copy(
            src_ref=src, dst_ref=dst, send_sem=ss, recv_sem=rs,
            device_id={axis: index}, device_id_type=MESH,
        )

    def forward(w):
        get_x[w].wait()
        base = w * step
        pre[base : base + step] = jnp.dot(
            x_v[w].reshape(step, depth), win_v[...], preferred_element_type=F32
        )

        @pl.loop(0, step // 16)
        def _(n):
            at = pl.ds(pl.multiple_of(base + n * 16, 16), 16)
            z = pre[at] + bin_ref[...]
            pre[at] = z
            t = jnp.tanh(z * (GELU_C + (GELU_C * GELU_A) * (z * z)))
            hz = 0.5 * z
            act[at] = (hz + hz * t).astype(BF16)

        value = jnp.dot(act[base : base + step], w128[...], preferred_element_type=F32)
        fsend[w] = value.reshape(M, pw, LANES).astype(BF16)
        if w == 0:
            pl.semaphore_wait(barrier, (M - 1) + (G - 1) + 1)
        frecv[w, pl.ds(me, 1)] = fsend[w, pl.ds(me, 1)]
        return spread(w, fsend, frecv, f_ss, f_rs)

    def spread(w, src, dst, ss, rs):
        copies = []
        for s in range(1, M):
            j = lax.rem(me + s, M)
            sem = w * M + s
            copy = remote(src.at[w, j], dst.at[w, me], ss.at[sem], rs.at[sem], "member", j)
            copy.start()
            copies.append(copy)
        return copies

    f_copies = [forward(0)]

    for n in range(tiles):
        get_t[n].wait()
        rest = jnp.zeros((LANES - fields - 1, LANES), F32)
        tt[n * LANES : (n + 1) * LANES] = jnp.concatenate(
            [tv[n], area_ref[pl.ds(tile + n, 1)], rest], axis=0
        ).T
    shift = me * per - tile * LANES
    bout = jnp.concatenate([bout_ref[...], jnp.zeros((1, LANES - fields), F32)], axis=1)
    var = jnp.concatenate([var_ref[...], jnp.zeros((1, LANES - fields), F32)], axis=1)
    eps_fair = (1.0 - alpha_fair) / M
    pairwise = (1.0 - eps_fair) / (M * (M - 1))
    loss_scale = M / math.sqrt(S * G * points)

    def pairs(w):
        for copy in f_copies[w]:
            copy.wait_recv()

        @pl.loop(0, pw // 16)
        def _(n):
            at = pl.ds(pl.multiple_of(n * 16, 16), 16)
            seen = tt[pl.ds(pl.multiple_of(shift + w * pw + n * 16, 16), 16)]
            scale = (loss_scale * seen[:, fields : fields + 1]) * var
            target = seen - bout
            f = [frecv[w, j, at].astype(F32) for j in range(M)]
            total = [jnp.zeros((16, LANES), F32) for _ in range(M)]
            for j in range(M):
                for k in range(j + 1, M):
                    slope = softened_slope(f[j] - f[k])
                    total[j] = total[j] + slope
                    total[k] = total[k] - slope
            for j in range(M):
                g = scale * (softened_slope(f[j] - target) * (1.0 / M) - pairwise * total[j])
                gsend[w, j, at] = g.astype(BF16)

        grecv[w, pl.ds(me, 1)] = gsend[w, pl.ds(me, 1)]
        return spread(w, gsend, grecv, g_ss, g_rs)

    f_copies = f_copies + [forward(w) for w in range(1, waves)]
    g_copies = [pairs(w) for w in range(waves)]

    @pl.loop(0, points // 16)
    def _(n):
        at = pl.ds(pl.multiple_of(n * 16, 16), 16)
        z = pre[at]
        q = z * z
        t = jnp.tanh(z * (GELU_C + (GELU_C * GELU_A) * q))
        inner = GELU_C + (3.0 * GELU_C * GELU_A) * q
        pre[at] = (0.5 + 0.5 * t) + (0.5 * z) * (1.0 - t * t) * inner

    for w in range(waves):
        xt_v[:, w * step : (w + 1) * step] = x_v[w].reshape(step, depth).T
    bias_acc[...] = jnp.zeros_like(bias_acc)

    for w in range(waves):
        for copy in g_copies[w]:
            copy.wait_recv()
        base = w * step
        rows = grecv[w].reshape(step, LANES)
        back = jnp.dot(rows, w128t[...], preferred_element_type=F32)
        pre[base : base + step] = pre[base : base + step] * back

        @pl.loop(0, step // 16)
        def _(n):
            at = pl.ds(pl.multiple_of(base + n * 16, 16), 16)
            value = pre[at]
            pg[at] = value.astype(BF16)
            bias_acc[...] += value[0:8] + value[8:16]

    goutt[...] = lax.dot_general(
        grecv[...].reshape(points, LANES), act[...], (((0,), (0,)), ((), ())),
        preferred_element_type=F32,
    )
    goutt[fields : fields + 1] = jnp.sum(bias_acc[...], axis=0, keepdims=True)
    chunks = half // LANES
    last = chunks
    kind = s1[0].dtype
    split = o_fin.shape[1] < R
    blocks = (G, MZ, MX, R, LANES)
    o_all[...] = goutt[...].T.reshape(o_all.shape)
    lengths = {"x": MX, "y": G, "z": MZ}
    index = {"x": mx, "y": grid, "z": mz}
    sem_base = {}
    sem_count = 0
    for n in range(chunks + 1):
        for stage in range(3):
            sem_base[(n, stage)] = sem_count
            sem_count += lengths[chunk_axes[n][stage]] - 1
    live = {}

    def peer(axis, to):
        if axis == "y":
            return "grid", to
        if axis == "x":
            return "member", mz * MX + to
        return "member", to * MX + mx

    def part(ref, axes, axis, to):
        where = [slice(None)] * len(axes)
        where[axes.index(axis)] = to
        return ref.at[tuple(where)]

    def send(n, stage, src, dst, axes):
        axis = chunk_axes[n][stage]
        started = []
        for s in range(1, lengths[axis]):
            to = lax.rem(index[axis] + s, lengths[axis])
            name, where = peer(axis, to)
            sem = sem_base[(n, stage)] + s - 1
            copy = remote(
                part(src, axes, axis, to), dst.at[s - 1], r_ss.at[sem], r_rs.at[sem], name, where
            )
            copy.start()
            started.append(copy)
        live[(n, stage)] = started

    c_copies = {}

    def exchange(n):
        copy = remote(csend[n], crecv[n], c_ss.at[n], c_rs.at[n], "sample", other)
        copy.start()
        c_copies[n] = copy

    def columns(n, owner):
        at = pl.ds(pl.multiple_of(owner * half + n * LANES, LANES), 2 * LANES)
        value = jnp.dot(xt_v[...], pg[:, at], preferred_element_type=F32)
        return [value[:, u * LANES : (u + 1) * LANES].reshape(blocks) for u in range(2)]

    def give(n):
        for u, value in enumerate(columns(n, other)):
            csend[n + u][...] = value.astype(kind)
            exchange(n + u)

    def keep(n):
        for u, value in enumerate(columns(n, core)):
            own[n + u][...] = value

    def first(n):
        c_copies[n].wait_recv()
        total = own[n][...] + crecv[n][...].astype(F32)
        own[n][...] = total
        s1[n][...] = total.astype(kind)
        send(n, 0, s1[n], r1[n], "yzx")

    def arrived(n, stage, kept, source):
        total = kept
        for s, copy in enumerate(live[(n, stage)]):
            copy.wait_recv()
            total = total + source[s].astype(F32)
        return total

    def second(n):
        axis = chunk_axes[n][0]
        kept = part(own[n], "yzx", axis, index[axis])[...]
        total = arrived(n, 0, kept, r1[n])
        acc[0][n][...] = total
        s2[n][...] = total.astype(kind)
        send(n, 1, s2[n], r2[n], "yzx".replace(axis, ""))

    def third(n):
        axes = "yzx".replace(chunk_axes[n][0], "")
        axis = chunk_axes[n][1]
        kept = part(acc[0][n], axes, axis, index[axis])[...]
        total = arrived(n, 1, kept, r2[n])
        acc[1][n][...] = total
        s3[n][...] = total.astype(kind)
        send(n, 2, s3[n], r3[n], axes.replace(axis, ""))

    e_copies = {}

    def finish(n):
        axis = chunk_axes[n][2]
        total = arrived(n, 2, acc[1][n][index[axis]], r3[n])
        if n == last:
            o_fin[core if split else 0] = total
            if not split:
                return
        else:
            at = pl.ds(pl.multiple_of(core * half + n * LANES, LANES), LANES)
            gin_ref[:, at] = total
        fin_s[n][...] = total
        copy = remote(fin_s[n], fin_r[n], e_ss.at[n], e_rs.at[n], "sample", other)
        copy.start()
        e_copies[n] = copy

    left = set()

    def gone(n, stage):
        for copy in live[(n, stage)]:
            copy.wait_send()
        left.add((n, stage))

    if split:
        csend[last][...] = o_all[:, :, :, other].astype(kind)
        own[last][...] = o_all[:, :, :, core]
    else:
        csend[last][...] = o_all[:, :, :, 0].astype(kind)
        own[last][...] = csend[last][...].astype(F32)
    exchange(last)
    give(0)
    first(last)
    keep(0)
    for n in (0, 1):
        first(n)
    for n in range(2, chunks, 2):
        give(n)
        keep(n)
    for n in range(2, chunks):
        gone(n - 2, 0)
        first(n)
    for stage, n in PLAN:
        (second, third)[stage](n)
    for n in (last, *range(chunks)):
        finish(n)
    for n in range(chunks):
        e_copies[n].wait_recv()
        at = pl.ds(pl.multiple_of(other * half + n * LANES, LANES), LANES)
        gin_ref[:, at] = fin_r[n][...]
    if split:
        e_copies[last].wait_recv()
        o_fin[other] = fin_r[last][...]
    total = o_fin[...].reshape(R, LANES)
    gout_ref[...] = total[:, 0:fields]
    gbias_ref[...] = total.T[fields : fields + 1, :]

    for copies in (*f_copies, *g_copies, c_copies.values(), e_copies.values()):
        for copy in copies:
            copy.wait_send()
    for key in live:
        if key not in left:
            gone(*key)


def hand_over(gin_ref, gbias_ref, gout_ref, gin_out, gbias_out, gout_out):
    gin_out[...] = gin_ref[...]
    gbias_out[...] = gbias_ref[...]
    gout_out[...] = gout_ref[...]


def local(
    sizes, hidden_states, targets, area_weight, var_weight, weight_in, bias_in, output_weight,
    output_bias,
):
    G, M, S = sizes
    MZ = MEMBER_ROWS
    MX = M // MZ
    points, depth = hidden_states.shape[2:]
    width, fields = output_weight.shape
    R = width // (G * M)
    per = points // M
    tiles = max(1, per // LANES)
    waves = 4
    pw = per // waves
    kind = BF16 if R % 16 == 0 else F32
    chunks = width // S // LANES
    chunk_axes = [ORDERS[n % 4] for n in range(chunks)] + [ORDERS[4]]
    lengths = {"x": MX, "y": G, "z": MZ}

    def dims(axes):
        return tuple(lengths[a] for a in axes)

    s1, r1, s2, r2, a2, s3, r3, a3, f32_own, fin = [], [], [], [], [], [], [], [], [], []
    sems = 0
    split = S == 2 and R % 32 == 0
    for n, axes in enumerate(chunk_axes):
        rows = R // 2 if split and n == chunks else R
        rest = "yzx".replace(axes[0], "")
        one = rest.replace(axes[1], "")
        tile = (rows, LANES)
        s1.append(pltpu.VMEM((*dims("yzx"), *tile), kind))
        f32_own.append(pltpu.VMEM((*dims("yzx"), *tile), F32))
        r1.append(pltpu.VMEM((lengths[axes[0]] - 1, *dims(rest), *tile), kind))
        s2.append(pltpu.VMEM((*dims(rest), *tile), kind))
        a2.append(pltpu.VMEM((*dims(rest), *tile), F32))
        r2.append(pltpu.VMEM((lengths[axes[1]] - 1, *dims(one), *tile), kind))
        s3.append(pltpu.VMEM((*dims(one), *tile), kind))
        a3.append(pltpu.VMEM((*dims(one), *tile), F32))
        r3.append(pltpu.VMEM((lengths[axes[2]] - 1, *tile), kind))
        fin.append(pltpu.VMEM(tile, F32))
        sems += sum(lengths[a] - 1 for a in axes)
    halves = 2 if split else 1
    o_all = pltpu.VMEM((G, MZ, MX, halves, R // halves, LANES), F32)
    o_fin = pltpu.VMEM((halves, R // halves, LANES), F32)
    dma = pltpu.SemaphoreType.DMA
    scratch = [
        pltpu.VMEM((waves, M, pw, depth), BF16),
        pltpu.VMEM((depth, points), BF16),
        pltpu.VMEM((depth, width), BF16),
        pltpu.VMEM((fields, width), BF16),
        pltpu.VMEM((width, LANES), BF16),
        pltpu.VMEM((LANES, width), BF16),
        pltpu.VMEM((tiles, fields, LANES), F32),
        pltpu.VMEM((tiles * LANES, LANES), F32),
        pltpu.VMEM((points, width), F32),
        pltpu.VMEM((points, width), BF16),
        pltpu.VMEM((points, width), BF16),
        pltpu.VMEM((8, width), F32),
        pltpu.VMEM((waves, M, pw, LANES), BF16),
        pltpu.VMEM((waves, M, pw, LANES), BF16),
        pltpu.VMEM((waves, M, pw, LANES), BF16),
        pltpu.VMEM((waves, M, pw, LANES), BF16),
        pltpu.VMEM((LANES, width), F32),
        s1, s1, f32_own, o_all, o_fin, s1, r1, s2, r2, s3, r3, [a2, a3], fin, fin,
        dma((2 + waves + tiles,)), *[dma((waves * M,))] * 4,
        dma((chunks + 1,)), dma((chunks + 1,)), dma((sems,)), dma((sems,)),
        dma((chunks + 1,)), dma((chunks + 1,)),
    ]
    flat, tree = jax.tree.flatten(scratch, is_leaf=lambda leaf: not isinstance(leaf, list))

    def body(*refs):
        head, tail = refs[:11], refs[11:]
        kernel(
            (G, MZ, MX, S, R), chunk_axes, *head, *jax.tree.unflatten(tree, tail)
        )

    whole = pl.BlockSpec(memory_space=pltpu.VMEM)
    anywhere = pl.BlockSpec(memory_space=pl.ANY)
    flops = 4 * points * depth * width + 6 * points * width * LANES
    gin, gbias, gout = pl.pallas_call(
        body,
        out_shape=(
            jax.ShapeDtypeStruct((R, width), F32),
            jax.ShapeDtypeStruct((1, R), F32),
            jax.ShapeDtypeStruct((R, fields), F32),
        ),
        in_specs=[anywhere, anywhere, whole, whole, anywhere, whole, anywhere, whole],
        out_specs=(whole, whole, whole),
        scratch_shapes=flat,
        compiler_params=pltpu.CompilerParams(
            collective_id=0, has_side_effects=True, vmem_limit_bytes=56 * 1024 * 1024
        ),
        cost_estimate=pl.CostEstimate(
            flops=flops, bytes_accessed=6 * 1024 * 1024, transcendentals=2 * points * width
        ),
        name="crps_gradient",
    )(
        hidden_states.reshape(M, waves, pw, depth), targets.reshape(fields, points // LANES, LANES),
        area_weight.reshape(points // LANES, LANES), var_weight[None], weight_in, bias_in[None],
        output_weight.T, output_bias[None],
    )
    gin, gbias, gout = pl.pallas_call(
        hand_over,
        out_shape=(
            jax.ShapeDtypeStruct((R, width), F32),
            jax.ShapeDtypeStruct((1, R), F32),
            jax.ShapeDtypeStruct((R, fields), F32),
        ),
        in_specs=[whole, whole, whole],
        out_specs=(whole, whole, whole),
        name="results",
    )(gin, gbias, gout)
    return gin, gbias.reshape(R), gout


def solution(mesh):
    placed = (
        P("sample", "member", "grid", None),
        P("sample", None, "grid"),
        P("grid"),
        P(),
        P(),
        P(),
        P(),
        P(),
    )
    sizes = (mesh.shape["grid"], mesh.shape["member"], mesh.shape["sample"])
    return jax.shard_map(
        functools.partial(local, sizes),
        mesh=mesh,
        in_specs=placed,
        out_specs=(P(("grid", "member"), None), P(("grid", "member")), P(("grid", "member"), None)),
        check_vma=False,
    )
```
